1024 devices in a mesh: dp: 64 (over z, core), expert: 16 (over y, x).
Axes of the slice: x: 4, y: 4, z: 32, core: 2. Of those that a mesh axis runs over, the one named last changes fastest.
Arguments:
- grads: bfloat16 [16, 64, 1024, 768], P('expert', 'dp'), may hold values from -3000 to 3000
- momentum: float32 [64, 1024, 768], P('dp', 'expert'), may hold values from -3000 to 3000
Outputs:
- update: bfloat16 [64, 1024, 768], P('dp', 'expert')
- new_momentum: float32 [64, 1024, 768], P('dp', 'expert')
The draws below stay inside these ranges and needn't reach their ends.
All inputs are finite; a program needn't handle non-finite values.
Results may differ from the reference program's by a relative error of at most 0.023.
Values may be sent and summed in bfloat16 or wider, within the bound.
No kernel may reach another device: no remote copies, remote signals or barrier semaphores. Data moves between devices by JAX's collectives and lax.ppermute only.
A program may use at most 32 MiB of HBM per device.

```python
import math
import jax
import jax.numpy as jnp
from jax import lax

D = 1024
R = 768
ITERS = 3
MATS = 64
N_EXPERT = 16


def scales(key, lead, count):
    first, second = jax.random.split(key)
    row_scale = jnp.exp(jax.random.uniform(first, (lead, count, D, 1), jnp.float32, 0.0, math.log(10.0)))
    col_scale = jnp.exp(jax.random.uniform(second, (1, count, 1, R), jnp.float32, 0.0, math.log(10.0)))
    row_block = jnp.arange(D) // (D // N_EXPERT)
    col_block = jnp.arange(R) // (R // N_EXPERT)
    boost = 1.0 + 4.0 * (row_block[:, None] == col_block[None, :]).astype(jnp.float32)
    return row_scale * col_scale * boost


def draw_grads(key, part):
    key = jax.random.fold_in(key, 11)
    first, second = jax.random.split(key, 2)
    shape = (N_EXPERT, MATS, D, R)
    base = jnp.clip(jax.random.normal(first, shape, jnp.float32), -4.0, 4.0)
    rise = 1.0 + 2.0 * jnp.arange(N_EXPERT, dtype=jnp.float32) / max(N_EXPERT - 1, 1)
    values = 0.3 * base * scales(second, N_EXPERT, MATS) * rise[:, None, None, None]
    return values.astype(jnp.bfloat16)


def draw_momentum(key, part):
    key = jax.random.fold_in(key, 23)
    first, second = jax.random.split(key)
    shape = (1, MATS, D, R)
    base = jnp.clip(jax.random.normal(first, shape, jnp.float32), -4.0, 4.0)
    values = 0.6 * base * scales(second, 1, MATS)
    return values[0].astype(jnp.float32)


def setup_inputs(seed: int = 0) -> dict:
    arg_keys = jax.random.split(jax.random.key(seed), 3)
    grads = draw_grads(jax.random.fold_in(arg_keys[2], 71), 0)
    momentum = draw_momentum(jax.random.fold_in(arg_keys[2], 71), 0)
    return dict(grads=grads, momentum=momentum)


rate = 0.95
eps = 1e-07
coef_a = 3.4445
coef_b = -4.775
coef_c = 2.0315

def orthogonalize(start):
    current = start
    for step in range(ITERS):
        wide = current.astype(jnp.float32)
        gram = jnp.einsum('dr,ds->rs', wide, wide).astype(jnp.bfloat16)
        square = jnp.dot(gram, gram, preferred_element_type=jnp.float32)
        poly = (coef_b * gram.astype(jnp.float32) + coef_c * square).astype(jnp.bfloat16)
        product = jnp.dot(current, poly, preferred_element_type=jnp.float32)
        current = (coef_a * current.astype(jnp.float32) + product).astype(jnp.bfloat16)
    return current

def one_matrix(pieces):
    terms, moment = pieces
    total = lax.optimization_barrier(jnp.sum(terms.astype(jnp.float32), axis=0))
    fresh = rate * moment + total
    blend = total + rate * fresh
    frob = jnp.sqrt(jnp.sum(blend * blend))
    iterate = (blend / (frob + eps)).astype(jnp.bfloat16)
    final = orthogonalize(iterate)
    factor = 0.2 * math.sqrt(max(D, R))
    return ((factor * final.astype(jnp.float32)).astype(jnp.bfloat16), fresh)

def reference(grads, momentum):
    terms = jnp.moveaxis(grads, 1, 0)
    update, new_momentum = lax.map(one_matrix, (terms, momentum))
    return (update, new_momentum)
```

```python
import functools
import math

import jax
import jax.numpy as jnp
from jax import lax
from jax.experimental import pallas as pl
from jax.experimental.pallas import tpu as pltpu
from jax.sharding import PartitionSpec as P

D = 1024
R = 768
ITERS = 3
N_EXPERT = 16
ROWS = D // N_EXPERT


rate = 0.95
eps = 1e-07
coef_a = 3.4445
coef_b = -4.775
coef_c = 2.0315
f32 = jnp.float32
bf16 = jnp.bfloat16


def dot(lhs, rhs, side=1):
    return lax.dot_general(lhs, rhs, (((side,), (0,)), ((), ())), preferred_element_type=f32)


def newton_schulz(whole_ref, own_ref, out_ref, wide, gram, poly, half, rows):
    wide[...] = dot(whole_ref[...], whole_ref[...], side=0)
    diagonal = lax.broadcasted_iota(jnp.int32, (R, R), 0) == lax.broadcasted_iota(jnp.int32, (R, R), 1)
    squares = jnp.full((1, 1), jnp.sum(jnp.where(diagonal, wide[...], 0.0)), f32)
    inverse = 1.0 / (jnp.sqrt(squares) + eps)
    gram[...] = (wide[...] * inverse * inverse).astype(bf16)
    rows[...] = own_ref[...]
    for step in range(ITERS):
        square = dot(gram[...], gram[...])
        poly[...] = (coef_b * gram[...].astype(f32) + coef_c * square).astype(bf16)
        if step < ITERS - 1:
            half[...] = (coef_a * gram[...].astype(f32) + dot(gram[...], poly[...])).astype(bf16)
            gram[...] = (coef_a * half[...].astype(f32) + dot(half[...], poly[...])).astype(bf16)
        moved = coef_a * rows[...].astype(f32) + dot(rows[...], poly[...])
        if step == 0:
            moved = moved * inverse
        rows[...] = moved.astype(bf16)
    factor = 0.2 * math.sqrt(max(D, R))
    out_ref[...] = (factor * rows[...].astype(f32)).astype(bf16)


def orthogonalize(whole, own):
    vmem = pl.BlockSpec(memory_space=pltpu.VMEM)
    return pl.pallas_call(
        newton_schulz,
        out_shape=jax.ShapeDtypeStruct((ROWS, R), bf16),
        in_specs=[vmem, vmem],
        out_specs=vmem,
        scratch_shapes=[
            pltpu.VMEM((R, R), f32),
            pltpu.VMEM((R, R), bf16),
            pltpu.VMEM((R, R), bf16),
            pltpu.VMEM((R, R), bf16),
            pltpu.VMEM((ROWS, R), bf16),
        ],
        compiler_params=pltpu.CompilerParams(vmem_limit_bytes=40 * 2**20),
    )(whole, own)


def exchange(blocks):
    return lax.all_to_all(blocks, "expert", 0, 0, tiled=True)


def shards(grads, momentum):
    terms = exchange(grads.reshape(N_EXPERT, ROWS, R))
    total = jnp.sum(terms.astype(f32), axis=0)
    new_momentum = rate * momentum[0] + total
    blend = (total + rate * new_momentum).astype(bf16)
    whole = exchange(jnp.broadcast_to(blend[None], (N_EXPERT, ROWS, R))).reshape(D, R)
    update = orthogonalize(whole, blend)
    return (update[None], new_momentum[None])


def solution(mesh):
    return jax.shard_map(
        shards,
        mesh=mesh,
        in_specs=(P("expert", "dp", None, None), P("dp", "expert", None)),
        out_specs=(P("dp", "expert", None), P("dp", "expert", None)),
        check_vma=False,
    )
```

```python
import functools
import math

import jax
import jax.numpy as jnp
from jax import lax
from jax.experimental import pallas as pl
from jax.experimental.pallas import tpu as pltpu
from jax.sharding import PartitionSpec as P

D = 1024
R = 768
N_EXPERT = 16
ROWS = D // N_EXPERT
SIDE = 4
TILE = 256


rate = 0.95
eps = 1e-07
coef_a = 3.4445
coef_b = -4.775
coef_c = 2.0315
share = rate * rate / (1 + rate)
f32 = jnp.float32
bf16 = jnp.bfloat16
VMEM = pl.BlockSpec(memory_space=pltpu.VMEM)
SMALL = pltpu.CompilerParams(vmem_limit_bytes=8 * 2**20)


def dot(lhs, rhs, side=1):
    return lax.dot_general(lhs, rhs, (((side,), (0,)), ((), ())), preferred_element_type=f32)


def mirror(target, column, value):
    cols = slice(column * TILE, (column + 1) * TILE)
    target[: (column + 1) * TILE, cols] = value
    for row in range(column):
        target[cols, row * TILE : (row + 1) * TILE] = jnp.transpose(value[row * TILE : (row + 1) * TILE, :])


def symmetric(target, lhs, rhs, linear, scale, factor):
    for column in range(R // TILE):
        cols, depth = slice(column * TILE, (column + 1) * TILE), (column + 1) * TILE
        product = dot(lhs[:depth, :], rhs[:, cols])
        mirror(target, column, (scale * linear[:depth, cols].astype(f32) + factor * product).astype(bf16))


def newton_schulz(whole_ref, out_ref, wide, gram, poly, half):
    squares = jnp.zeros((1, 1), f32)
    diagonal = lax.broadcasted_iota(jnp.int32, (TILE, TILE), 0) == lax.broadcasted_iota(jnp.int32, (TILE, TILE), 1)
    for column in range(R // TILE):
        cols, depth = slice(column * TILE, (column + 1) * TILE), (column + 1) * TILE
        wide[:depth, cols] = dot(whole_ref[:, :depth], whole_ref[:, cols], side=0)
        squares += jnp.sum(jnp.where(diagonal, wide[cols, cols], 0.0))
    inverse = 1.0 / (jnp.sqrt(squares) + eps / (1 + rate))
    for column in range(R // TILE):
        cols, depth = slice(column * TILE, (column + 1) * TILE), (column + 1) * TILE
        mirror(gram, column, (wide[:depth, cols] * inverse * inverse).astype(bf16))

    symmetric(poly, gram, gram, gram, coef_b, coef_c)
    symmetric(half, gram, poly, gram, coef_a, 1.0)
    expert, start = lax.axis_index("expert"), place() * ROWS
    start += jnp.where(lax.axis_index("dp") % 2 == 0, expert % SIDE, expert // SIDE) * SIDE * ROWS
    rows = whole_ref[pl.ds(pl.multiple_of(start, ROWS), ROWS), :]
    rows = (inverse * (coef_a * rows.astype(f32) + dot(rows, poly[...]))).astype(bf16)
    symmetric(gram, half, poly, half, coef_a, 1.0)
    symmetric(poly, gram, gram, gram, coef_b, coef_c)

    def step(value):
        return (coef_a * value.astype(f32) + dot(value, poly[...])).astype(bf16)

    def last_gram(value):
        return dot(step(step(value)), gram[...])

    rows = step(rows)
    once = last_gram(rows)
    twice = last_gram(once.astype(bf16))
    rows = (coef_a * rows.astype(f32) + coef_b * once + coef_c * twice).astype(bf16)
    factor = 0.2 * math.sqrt(max(D, R))
    out_ref[...] = (factor * rows.astype(f32)).astype(bf16)


def orthogonalize(whole):
    return pl.pallas_call(
        newton_schulz,
        out_shape=jax.ShapeDtypeStruct((ROWS, R), bf16),
        in_specs=[VMEM],
        out_specs=VMEM,
        scratch_shapes=[
            pltpu.VMEM((R, R), f32),
            pltpu.VMEM((R, R), bf16),
            pltpu.VMEM((R, R), bf16),
            pltpu.VMEM((R, R), bf16),
        ],
        compiler_params=pltpu.CompilerParams(vmem_limit_bytes=20 * 2**20),
    )(whole)


def place():
    expert = lax.axis_index("expert")
    return jnp.where(lax.axis_index("dp") % 2 == 0, expert // SIDE, expert % SIDE)


def order(grads):
    along_x = lax.axis_index("dp") % 2 == 0
    tiles = grads.reshape(SIDE, SIDE, ROWS, R)
    return lax.cond(along_x, lambda t: jnp.swapaxes(t, 0, 1), lambda t: t, tiles)


def partial_kernel(terms_ref, momentum_ref, sent_ref, own_ref):
    mine = place()
    for sub in range(SIDE):
        total = sum(terms_ref[peer, sub].astype(f32) for peer in range(SIDE))
        weight = jnp.where(mine == sub, share, 0.0).astype(f32)
        sent = (total + weight * momentum_ref[...]).astype(bf16)
        for peer in range(SIDE):
            sent_ref[peer, sub] = sent
    own_ref[...] = sum(terms_ref[peer, mine].astype(f32) for peer in range(SIDE))


def partial_sums(terms, momentum):
    return pl.pallas_call(
        partial_kernel,
        out_shape=(jax.ShapeDtypeStruct((SIDE, SIDE, ROWS, R), bf16), jax.ShapeDtypeStruct((ROWS, R), f32)),
        in_specs=[VMEM, VMEM],
        out_specs=(VMEM, VMEM),
        compiler_params=SMALL,
    )(terms, momentum)


def blend_kernel(got_ref, own_ref, sent_ref, total_ref):
    mine = place()
    for sub in range(SIDE):
        blend = sum(got_ref[peer, sub].astype(f32) for peer in range(SIDE)).astype(bf16)
        for peer in range(SIDE):
            sent_ref[peer, sub] = blend
    total_ref[...] = own_ref[...] + sum(
        jnp.where(mine == peer, 0.0, 1.0).astype(f32) * got_ref[peer, mine].astype(f32) for peer in range(SIDE)
    )


def blends(got, own):
    return pl.pallas_call(
        blend_kernel,
        out_shape=(jax.ShapeDtypeStruct((SIDE, SIDE, ROWS, R), bf16), jax.ShapeDtypeStruct((ROWS, R), f32)),
        in_specs=[VMEM, VMEM],
        out_specs=(VMEM, VMEM),
        compiler_params=SMALL,
    )(got, own)


def exchange(blocks, groups):
    return lax.all_to_all(blocks, ("dp", "expert"), 0, 0, tiled=True, axis_index_groups=groups)


def lines(count, first):
    groups = []
    for dp in range(count):
        for fixed in range(SIDE):
            along_x = [fixed * SIDE + moving for moving in range(SIDE)]
            along_y = [moving * SIDE + fixed for moving in range(SIDE)]
            groups.append([dp * N_EXPERT + e for e in (along_x if dp % 2 == first else along_y)])
    return groups


def shards(count, grads, momentum):
    first, second = lines(count, 0), lines(count, 1)
    terms = exchange(order(grads), first)
    sent, own = partial_sums(terms, momentum[0])
    sent, total = blends(exchange(sent, second), own)
    whole = exchange(sent, first).reshape(D, R)
    new_momentum = rate * momentum[0] + total
    return (orthogonalize(whole)[None], new_momentum[None])


def solution(mesh):
    return jax.shard_map(
        functools.partial(shards, mesh.shape["dp"]),
        mesh=mesh,
        in_specs=(P("expert", "dp", None, None), P("dp", "expert", None)),
        out_specs=(P("dp", "expert", None), P("dp", "expert", None)),
        check_vma=False,
    )
```

```python
import math

import jax
import jax.numpy as jnp
from jax import lax
from jax.experimental import pallas as pl
from jax.experimental.pallas import tpu as pltpu
from jax.sharding import PartitionSpec as P

D = 1024
R = 768
N_EXPERT = 16
ROWS = D // N_EXPERT
TILE = 256


rate = 0.95
eps = 1e-07
coef_a = 3.4445
coef_b = -4.775
coef_c = 2.0315
f32 = jnp.float32
bf16 = jnp.bfloat16
VMEM = pl.BlockSpec(memory_space=pltpu.VMEM)
SMALL = pltpu.CompilerParams(vmem_limit_bytes=8 * 2**20)


def dot(lhs, rhs, side=1):
    return lax.dot_general(lhs, rhs, (((side,), (0,)), ((), ())), preferred_element_type=f32)


def mirror(target, column, value):
    cols = slice(column * TILE, (column + 1) * TILE)
    target[: (column + 1) * TILE, cols] = value
    for row in range(column):
        target[cols, row * TILE : (row + 1) * TILE] = jnp.transpose(value[row * TILE : (row + 1) * TILE, :])


def symmetric(target, lhs, rhs, linear, scale, factor):
    for column in range(R // TILE):
        cols, depth = slice(column * TILE, (column + 1) * TILE), (column + 1) * TILE
        product = dot(lhs[:depth, :], rhs[:, cols])
        mirror(target, column, (scale * linear[:depth, cols].astype(f32) + factor * product).astype(bf16))


def newton_schulz(whole_ref, total_ref, momentum_ref, out_ref, new_ref, wide, gram, poly, half, fresh, sem):
    fresh[...] = rate * momentum_ref[...] + total_ref[...]
    leave = pltpu.make_async_copy(fresh, new_ref, sem)
    leave.start()

    squares = jnp.zeros((1, 1), f32)
    diagonal = lax.broadcasted_iota(jnp.int32, (TILE, TILE), 0) == lax.broadcasted_iota(jnp.int32, (TILE, TILE), 1)
    for column in range(R // TILE):
        cols, depth = slice(column * TILE, (column + 1) * TILE), (column + 1) * TILE
        wide[:depth, cols] = dot(whole_ref[:, :depth], whole_ref[:, cols], side=0)
        squares += jnp.sum(jnp.where(diagonal, wide[cols, cols], 0.0))
    inverse = 1.0 / (jnp.sqrt(squares) + eps)
    for column in range(R // TILE):
        cols, depth = slice(column * TILE, (column + 1) * TILE), (column + 1) * TILE
        mirror(gram, column, (wide[:depth, cols] * inverse * inverse).astype(bf16))

    symmetric(poly, gram, gram, gram, coef_b, coef_c)
    symmetric(half, gram, poly, gram, coef_a, 1.0)
    start = pl.multiple_of(lax.axis_index("expert") * ROWS, ROWS)
    rows = whole_ref[pl.ds(start, ROWS), :]
    rows = (inverse * (coef_a * rows.astype(f32) + dot(rows, poly[...]))).astype(bf16)
    symmetric(gram, half, poly, half, coef_a, 1.0)
    symmetric(poly, gram, gram, gram, coef_b, coef_c)

    def step(value):
        return (coef_a * value.astype(f32) + dot(value, poly[...])).astype(bf16)

    def last_gram(value):
        return dot(step(step(value)), gram[...])

    rows = step(rows)
    once = last_gram(rows)
    twice = last_gram(once.astype(bf16))
    rows = (coef_a * rows.astype(f32) + coef_b * once + coef_c * twice).astype(bf16)
    factor = 0.2 * math.sqrt(max(D, R))
    out_ref[...] = (factor * rows.astype(f32)).astype(bf16)
    leave.wait()


def orthogonalize(whole, total, momentum):
    return pl.pallas_call(
        newton_schulz,
        out_shape=(jax.ShapeDtypeStruct((ROWS, R), bf16), jax.ShapeDtypeStruct((ROWS, R), f32)),
        in_specs=[VMEM, VMEM, VMEM],
        out_specs=(VMEM, pl.BlockSpec(memory_space=pl.ANY)),
        scratch_shapes=[
            pltpu.VMEM((R, R), f32),
            pltpu.VMEM((R, R), bf16),
            pltpu.VMEM((R, R), bf16),
            pltpu.VMEM((R, R), bf16),
            pltpu.VMEM((ROWS, R), f32),
            pltpu.SemaphoreType.DMA,
        ],
        compiler_params=pltpu.CompilerParams(vmem_limit_bytes=20 * 2**20),
    )(whole, total, momentum)


def blend_kernel(terms_ref, momentum_ref, sent_ref, total_ref):
    total = sum(terms_ref[peer].astype(f32) for peer in range(N_EXPERT))
    total_ref[...] = total
    blend = (total + rate * (rate * momentum_ref[...] + total)).astype(bf16)
    for peer in range(N_EXPERT):
        sent_ref[peer] = blend


def blends(terms, momentum):
    return pl.pallas_call(
        blend_kernel,
        out_shape=(jax.ShapeDtypeStruct((N_EXPERT, ROWS, R), bf16), jax.ShapeDtypeStruct((ROWS, R), f32)),
        in_specs=[VMEM, VMEM],
        out_specs=(VMEM, VMEM),
        compiler_params=SMALL,
    )(terms, momentum)


def exchange(blocks):
    return lax.all_to_all(blocks, "expert", 0, 0, tiled=True)


def shards(grads, momentum):
    sent, total = blends(exchange(grads.reshape(N_EXPERT, ROWS, R)), momentum[0])
    update, new_momentum = orthogonalize(exchange(sent).reshape(D, R), total, momentum[0])
    return (update[None], new_momentum[None])


def solution(mesh):
    return jax.shard_map(
        shards,
        mesh=mesh,
        in_specs=(P("expert", "dp", None, None), P("dp", "expert", None)),
        out_specs=(P("dp", "expert", None), P("dp", "expert", None)),
        check_vma=False,
    )
```

```python
import math

import jax
import jax.numpy as jnp
from jax import lax
from jax.experimental import pallas as pl
from jax.experimental.pallas import tpu as pltpu
from jax.sharding import PartitionSpec as P

D = 1024
R = 768
N_EXPERT = 16
ROWS = D // N_EXPERT
TILE = 256


rate = 0.95
eps = 1e-07
coef_a = 3.4445
coef_b = -4.775
coef_c = 2.0315
f32 = jnp.float32
bf16 = jnp.bfloat16
VMEM = pl.BlockSpec(memory_space=pltpu.VMEM)
SMALL = pltpu.CompilerParams(vmem_limit_bytes=8 * 2**20)


def dot(lhs, rhs, side=1):
    return lax.dot_general(lhs, rhs, (((side,), (0,)), ((), ())), preferred_element_type=f32)


def mirror(target, column, value):
    cols = slice(column * TILE, (column + 1) * TILE)
    target[: (column + 1) * TILE, cols] = value
    for row in range(column):
        target[cols, row * TILE : (row + 1) * TILE] = jnp.transpose(value[row * TILE : (row + 1) * TILE, :])


def symmetric(target, lhs, rhs, linear, scale, factor):
    for column in range(R // TILE):
        cols, depth = slice(column * TILE, (column + 1) * TILE), (column + 1) * TILE
        product = dot(lhs[:depth, :], rhs[:, cols])
        mirror(target, column, (scale * linear[:depth, cols].astype(f32) + factor * product).astype(bf16))


def newton_schulz(whole_ref, fresh_ref, out_ref, new_ref, gram, poly, half, sem):
    leave = pltpu.make_async_copy(fresh_ref, new_ref, sem)
    leave.start()

    squares = jnp.zeros((ROWS, R), f32)
    for block in range(N_EXPERT):
        part = whole_ref[block * ROWS : (block + 1) * ROWS, :].astype(f32)
        squares += part * part
    inverse = 1.0 / (jnp.sqrt(jnp.full((1, 1), jnp.sum(squares), f32)) + eps)
    for column in range(R // TILE):
        cols, depth = slice(column * TILE, (column + 1) * TILE), (column + 1) * TILE
        product = dot(whole_ref[:, :depth], whole_ref[:, cols], side=0)
        mirror(gram, column, (product * (inverse * inverse)).astype(bf16))

    symmetric(poly, gram, gram, gram, coef_b, coef_c)
    symmetric(half, gram, poly, gram, coef_a, 1.0)
    start = pl.multiple_of(lax.axis_index("expert") * ROWS, ROWS)
    rows = whole_ref[pl.ds(start, ROWS), :]
    rows = (inverse * (coef_a * rows.astype(f32) + dot(rows, poly[...]))).astype(bf16)
    symmetric(gram, half, poly, half, coef_a, 1.0)
    symmetric(poly, gram, gram, gram, coef_b, coef_c)

    def step(value):
        return (coef_a * value.astype(f32) + dot(value, poly[...])).astype(bf16)

    def last_gram(value):
        return dot(step(step(value)), gram[...])

    rows = step(rows)
    once = last_gram(rows)
    twice = last_gram(once.astype(bf16))
    rows = (coef_a * rows.astype(f32) + coef_b * once + coef_c * twice).astype(bf16)
    factor = 0.2 * math.sqrt(max(D, R))
    out_ref[...] = (factor * rows.astype(f32)).astype(bf16)
    leave.wait()


def orthogonalize(whole, fresh):
    return pl.pallas_call(
        newton_schulz,
        out_shape=(jax.ShapeDtypeStruct((ROWS, R), bf16), jax.ShapeDtypeStruct((ROWS, R), f32)),
        in_specs=[VMEM, VMEM],
        out_specs=(VMEM, pl.BlockSpec(memory_space=pl.ANY)),
        scratch_shapes=[
            pltpu.VMEM((R, R), bf16),
            pltpu.VMEM((R, R), bf16),
            pltpu.VMEM((R, R), bf16),
            pltpu.SemaphoreType.DMA,
        ],
        compiler_params=pltpu.CompilerParams(vmem_limit_bytes=20 * 2**20),
    )(whole, fresh)


def blend_kernel(terms_ref, momentum_ref, sent_ref, fresh_ref):
    total = sum(terms_ref[peer].astype(f32) for peer in range(N_EXPERT))
    fresh = rate * momentum_ref[...] + total
    fresh_ref[...] = fresh
    blend = (total + rate * fresh).astype(bf16)
    for peer in range(N_EXPERT):
        sent_ref[peer] = blend


def blends(terms, momentum):
    return pl.pallas_call(
        blend_kernel,
        out_shape=(jax.ShapeDtypeStruct((N_EXPERT, ROWS, R), bf16), jax.ShapeDtypeStruct((ROWS, R), f32)),
        in_specs=[VMEM, VMEM],
        out_specs=(VMEM, VMEM),
        compiler_params=SMALL,
    )(terms, momentum)


def exchange(blocks):
    return lax.all_to_all(blocks, "expert", 0, 0, tiled=True)


def shards(grads, momentum):
    sent, fresh = blends(exchange(grads.reshape(N_EXPERT, ROWS, R)), momentum[0])
    update, new_momentum = orthogonalize(exchange(sent).reshape(D, R), fresh)
    return (update[None], new_momentum[None])


def solution(mesh):
    return jax.shard_map(
        shards,
        mesh=mesh,
        in_specs=(P("expert", "dp", None, None), P("dp", "expert", None)),
        out_specs=(P("dp", "expert", None), P("dp", "expert", None)),
        check_vma=False,
    )
```

```python
import functools
import math

import jax
import jax.numpy as jnp
from jax import lax
from jax.experimental import pallas as pl
from jax.experimental.pallas import tpu as pltpu
from jax.sharding import PartitionSpec as P

D = 1024
R = 768
N_EXPERT = 16
ROWS = D // N_EXPERT
TILE = 256


rate = 0.95
eps = 1e-07
coef_a = 3.4445
coef_b = -4.775
coef_c = 2.0315
f32 = jnp.float32
bf16 = jnp.bfloat16
VMEM = pl.BlockSpec(memory_space=pltpu.VMEM)
SMALL = pltpu.CompilerParams(vmem_limit_bytes=8 * 2**20)


def dot(lhs, rhs, side=1):
    return lax.dot_general(lhs, rhs, (((side,), (0,)), ((), ())), preferred_element_type=f32)


def mirror(target, column, value):
    cols = slice(column * TILE, (column + 1) * TILE)
    target[: (column + 1) * TILE, cols] = value
    for row in range(column):
        target[cols, row * TILE : (row + 1) * TILE] = jnp.transpose(value[row * TILE : (row + 1) * TILE, :])


def symmetric(target, lhs, rhs, linear, scale, factor):
    for column in range(R // TILE):
        cols, depth = slice(column * TILE, (column + 1) * TILE), (column + 1) * TILE
        product = dot(lhs[:depth, :], rhs[:, cols])
        mirror(target, column, (scale * linear[:depth, cols].astype(f32) + factor * product).astype(bf16))


def newton_schulz(whole_ref, fresh_ref, out_ref, new_ref, gram, poly, half, sem):
    leave = pltpu.make_async_copy(fresh_ref, new_ref, sem)
    leave.start()

    squares = jnp.zeros((ROWS, R), f32)
    for block in range(N_EXPERT):
        part = whole_ref[block * ROWS : (block + 1) * ROWS, :].astype(f32)
        squares += part * part
    inverse = 1.0 / (jnp.sqrt(jnp.full((1, 1), jnp.sum(squares), f32)) + eps)
    for column in range(R // TILE):
        cols, depth = slice(column * TILE, (column + 1) * TILE), (column + 1) * TILE
        product = dot(whole_ref[:, :depth], whole_ref[:, cols], side=0)
        mirror(gram, column, (product * (inverse * inverse)).astype(bf16))

    symmetric(poly, gram, gram, gram, coef_b, coef_c)
    symmetric(half, gram, poly, gram, coef_a, 1.0)
    expert = lax.axis_index("expert")
    position = jnp.where(lax.axis_index("dp") % 2 == 0, expert, N_EXPERT - 1 - expert)
    start = pl.multiple_of(position * ROWS, ROWS)
    rows = whole_ref[pl.ds(start, ROWS), :]
    rows = (inverse * (coef_a * rows.astype(f32) + dot(rows, poly[...]))).astype(bf16)
    symmetric(gram, half, poly, half, coef_a, 1.0)
    symmetric(poly, gram, gram, gram, coef_b, coef_c)

    def step(value):
        return (coef_a * value.astype(f32) + dot(value, poly[...])).astype(bf16)

    def last_gram(value):
        return dot(step(step(value)), gram[...])

    rows = step(rows)
    once = last_gram(rows)
    twice = last_gram(once.astype(bf16))
    rows = (coef_a * rows.astype(f32) + coef_b * once + coef_c * twice).astype(bf16)
    factor = 0.2 * math.sqrt(max(D, R))
    out_ref[...] = (factor * rows.astype(f32)).astype(bf16)
    leave.wait()


def orthogonalize(whole, fresh):
    return pl.pallas_call(
        newton_schulz,
        out_shape=(jax.ShapeDtypeStruct((ROWS, R), bf16), jax.ShapeDtypeStruct((ROWS, R), f32)),
        in_specs=[VMEM, VMEM],
        out_specs=(VMEM, pl.BlockSpec(memory_space=pl.ANY)),
        scratch_shapes=[
            pltpu.VMEM((R, R), bf16),
            pltpu.VMEM((R, R), bf16),
            pltpu.VMEM((R, R), bf16),
            pltpu.SemaphoreType.DMA,
        ],
        compiler_params=pltpu.CompilerParams(vmem_limit_bytes=20 * 2**20),
    )(whole, fresh)


def blend_kernel(terms_ref, momentum_ref, sent_ref, fresh_ref):
    total = sum(terms_ref[peer].astype(f32) for peer in range(N_EXPERT))
    fresh = rate * momentum_ref[...] + total
    fresh_ref[...] = fresh
    blend = (total + rate * fresh).astype(bf16)
    for peer in range(N_EXPERT):
        sent_ref[peer] = blend


def blends(terms, momentum):
    return pl.pallas_call(
        blend_kernel,
        out_shape=(jax.ShapeDtypeStruct((N_EXPERT, ROWS, R), bf16), jax.ShapeDtypeStruct((ROWS, R), f32)),
        in_specs=[VMEM, VMEM],
        out_specs=(VMEM, VMEM),
        compiler_params=SMALL,
    )(terms, momentum)


def exchange(blocks):
    return lax.all_to_all(blocks, "expert", 0, 0, tiled=True)


def spread(blocks, count):
    order = range(N_EXPERT)
    groups = [[dp * N_EXPERT + e for e in (order if dp % 2 == 0 else order[::-1])] for dp in range(count)]
    return lax.all_to_all(blocks, ("dp", "expert"), 0, 0, tiled=True, axis_index_groups=groups)


def shards(count, grads, momentum):
    sent, fresh = blends(exchange(grads.reshape(N_EXPERT, ROWS, R)), momentum[0])
    update, new_momentum = orthogonalize(spread(sent, count).reshape(D, R), fresh)
    return (update[None], new_momentum[None])


def solution(mesh):
    return jax.shard_map(
        functools.partial(shards, mesh.shape["dp"]),
        mesh=mesh,
        in_specs=(P("expert", "dp", None, None), P("dp", "expert", None)),
        out_specs=(P("dp", "expert", None), P("dp", "expert", None)),
        check_vma=False,
    )
```
